32 devices in a mesh: groups: 2 (over y), replica: 2 (over core), tensor: 8 (over z, x).
Axes of the slice: x: 2, y: 2, z: 4, core: 2. Of those that a mesh axis runs over, the one named last changes fastest.
Arguments:
- query: bfloat16 [32, 8192], P(('groups', 'replica'), 'tensor'), parts along dimension 0, may hold values from -120 to 120
- key_cache_rows: bfloat16 [32, 8, 256, 128], P(('groups', 'replica'), None, 'tensor'), parts along dimension 0, may hold values from -6 to 6
- value_cache_rows: bfloat16 [32, 8, 256, 128], P(('groups', 'replica'), None, 'tensor'), parts along dimension 0, may hold values from -48 to 48
- cache_length: int32 [32], P(('groups', 'replica')), parts along dimension 0, may hold values from 2 to 256
- output_weight: bfloat16 [8192, 8192], P('tensor'), may hold values from -0.0625 to 0.0625
- adapter_down_weight: bfloat16 [256, 64, 8192], P('replica', None, 'tensor'), may hold values from -0.0625 to 0.0625
- adapter_up_weight: bfloat16 [256, 64, 8192], P('replica', None, 'tensor'), may hold values from -0.75 to 0.75
- slot_adapter_table: int32 [64], P('groups'), parts along dimension 0, may hold values from 0 to 255, as said below
- request_slot: int32 [32], P(('groups', 'replica')), parts along dimension 0, may hold values from 0 to 15
Outputs:
- mixed: bfloat16 [32, 8192], P(('groups', 'replica'), 'tensor'), parts along dimension 0
The draws below stay inside these ranges and needn't reach their ends.
There are 2 independent parts, one for each index of `groups`. The reference program is written for one: setup_inputs(seed, part) draws one part's arguments, and reference() takes and returns one part's arrays. A program takes and returns all parts, laid end to end along the dimension named above; an argument that names none is the same for every part. Nothing has to cross between parts.
Inputs may be any that keep to these rules, and one draw needn't show every extreme that they name: `slot_adapter_table`: the 16 adapters of one replica's slots are distinct.
All inputs are finite; a program needn't handle non-finite values.
Results may differ from the reference program's by a relative error of at most 0.015.
Values may be sent and summed in bfloat16 or wider, within the bound.
A program may use at most 192 MiB of HBM per device.

```python
import math
import jax
import jax.numpy as jnp
import numpy as np
from jax import lax

MODEL_WIDTH = 8192
QUERY_HEADS = 64
KVH = 8
HEAD_WIDTH = 128
ADAPTER_RANK = 64
SLOTS = 16
REQ = 8
TOKENS = 16
CTX = 256
ADAPTER_TOTAL = 256
N_REPLICA = 2


def cache_keys(key):
    return jax.random.truncated_normal(key, -6.0, 6.0, (TOKENS, KVH, CTX, HEAD_WIDTH), jnp.float32)


def draw_key_cache_rows(key, part):
    keys = cache_keys(key)
    return keys.astype(jnp.bfloat16)


def draw_query(key, part):
    key = jax.random.fold_in(key, 5)
    values = jax.random.truncated_normal(key, -6.0, 6.0, (TOKENS, QUERY_HEADS * HEAD_WIDTH), jnp.float32)
    return values.astype(jnp.bfloat16)


def draw_cache_length(key, part):
    key = jax.random.fold_in(key, 7)
    lengths = jax.random.randint(key, (TOKENS,), 2, CTX + 1, jnp.int32)
    return lengths.at[:4].set(CTX).astype(jnp.int32)


def draw_slot_adapter_table(key, part):
    key = jax.random.fold_in(key, 9)
    order = jax.random.permutation(key, ADAPTER_TOTAL).astype(jnp.int32)
    popular = order[:SLOTS // 2]
    others = order[SLOTS // 2:]
    blocks = []
    for which in range(N_REPLICA):
        mixed_order = jax.random.permutation(jax.random.fold_in(key, 100 + which), others)
        blocks.append(jnp.concatenate([popular, mixed_order[:SLOTS - SLOTS // 2]]))
    return jnp.concatenate(blocks).astype(jnp.int32)


def plant(result, stream_key, smallest, top_value):
    longest = result.shape.index(max(result.shape))
    spots = []
    for shift in (0, 1):
        where = [jax.random.randint(jax.random.fold_in(stream_key, axis), (), 0, length) for axis, length in enumerate(result.shape)]
        where[longest] = (where[longest] + shift) % result.shape[longest]
        spots.append(tuple(where))
    return result.at[spots[0]].set(smallest).at[spots[1]].set(top_value)


def block_levels(key, shape, cuts, least, high):
    def one(dim, shards_of):
        steps = jax.random.uniform(jax.random.fold_in(jax.random.fold_in(key, 6), dim), (shards_of,), jnp.float32, least / len(cuts), high / len(cuts))
        return jnp.repeat(jnp.exp(steps), shape[dim] // shards_of).reshape((-1,) + (1,) * (len(shape) - dim - 1))

    gain = one(*cuts[0])
    for cut in cuts[1:]:
        gain = gain * one(*cut)
    return gain


def cumulative_ranks(amount, slope):
    portions = [(1 << 20) // math.isqrt(standing ** slope) + 1 for standing in range(1, amount + 1)]
    deviation = 1 + sum(portions) // (1 << 30)
    return np.cumsum(np.array([max(1, weight // deviation) for weight in portions]))


def skewed_ids(rng, extent, number_of, skew):
    table = cumulative_ranks(number_of, skew)
    lot = jax.random.randint(jax.random.fold_in(rng, 1), extent, 0, int(table[number_of - 1]))
    rank = jnp.searchsorted(jnp.asarray(table, jnp.int32), lot, side="right")
    return jax.random.permutation(jax.random.fold_in(rng, 2), number_of)[rank].astype(jnp.int32)


def centred(key, shape, spread, most, cuts=(), kind=jnp.bfloat16):
    loudness = block_levels(key, shape, cuts, -0.22, 0.18) if cuts else 1.0
    entries = jax.random.normal(key, shape, jnp.float32) * spread * loudness
    return jnp.minimum(jnp.maximum(entries, -most), most).astype(kind)


def setup_inputs(seed: int = 0, part: int = 0) -> dict:
    splits = jax.random.split(jax.random.key(seed), 10)
    part_splits = jax.random.split(jax.random.fold_in(splits[9], part), 10)
    query = draw_query(jax.random.fold_in(jax.random.fold_in(splits[9], part), 71), part)
    key_cache_rows = draw_key_cache_rows(jax.random.fold_in(jax.random.fold_in(splits[9], part), 71), part)
    value_cache_rows = centred(part_splits[2], (TOKENS, KVH, CTX, HEAD_WIDTH), 8.0, 48.0, ((0, 2), (2, 8)))
    cache_length = draw_cache_length(jax.random.fold_in(jax.random.fold_in(splits[9], part), 71), part)
    output_weight = centred(splits[4], (QUERY_HEADS * HEAD_WIDTH, MODEL_WIDTH), (QUERY_HEADS * HEAD_WIDTH) ** -0.5, 0.0625, ((0, 8),))
    adapter_down_weight = centred(splits[5], (ADAPTER_TOTAL, ADAPTER_RANK, QUERY_HEADS * HEAD_WIDTH), (QUERY_HEADS * HEAD_WIDTH) ** -0.5, 0.0625, ((0, 2), (2, 8)))
    adapter_up_weight = centred(splits[6], (ADAPTER_TOTAL, ADAPTER_RANK, MODEL_WIDTH), ADAPTER_RANK ** -0.5, 0.75, ((0, 2), (2, 8)))
    slot_adapter_table = draw_slot_adapter_table(jax.random.fold_in(jax.random.fold_in(splits[9], part), 71), part)
    request_slot = plant(skewed_ids(part_splits[8], (TOKENS,), SLOTS, 2), jax.random.fold_in(part_splits[8], 3), 0, SLOTS - 1).astype(jnp.int32)
    return {"query": query, "key_cache_rows": key_cache_rows, "value_cache_rows": value_cache_rows, "cache_length": cache_length, "output_weight": output_weight, "adapter_down_weight": adapter_down_weight, "adapter_up_weight": adapter_up_weight, "slot_adapter_table": slot_adapter_table, "request_slot": request_slot}


def attend_one(args):
    query_row, keys, values, length = args
    group = QUERY_HEADS // KVH
    heads = query_row.astype(jnp.float32).reshape(KVH, group, HEAD_WIDTH)
    score = jnp.einsum('kgd,kcd->kgc', heads, keys.astype(jnp.float32)) / jnp.sqrt(jnp.float32(HEAD_WIDTH))
    live = (jnp.arange(CTX, dtype=jnp.int32) < length)[None, None, :]
    masked = jnp.where(live, score, jnp.float32(-1e+30))
    top = lax.optimization_barrier(jnp.max(masked, axis=2, keepdims=True))
    expo = jnp.where(live, jnp.exp(masked - top), jnp.float32(0.0))
    total = lax.optimization_barrier(jnp.sum(expo, axis=2))
    weight = expo.astype(jnp.bfloat16)
    summed = jnp.einsum('kgc,kcd->kgd', weight.astype(jnp.float32), values.astype(jnp.float32))
    return (summed / total[:, :, None]).reshape(QUERY_HEADS * HEAD_WIDTH).astype(jnp.bfloat16)

def reference(query, key_cache_rows, value_cache_rows, cache_length, output_weight, adapter_down_weight, adapter_up_weight, slot_adapter_table, request_slot):
    attention_output = lax.map(attend_one, (query, key_cache_rows, value_cache_rows, cache_length))
    base = jnp.dot(attention_output, output_weight, preferred_element_type=jnp.float32)
    replica_of = (jnp.arange(TOKENS, dtype=jnp.int32) // REQ).astype(jnp.int32)
    adapter_index = slot_adapter_table[replica_of * SLOTS + request_slot]
    down_factor_rows = adapter_down_weight[adapter_index]
    up_factor_rows = adapter_up_weight[adapter_index]
    reduced_features = jnp.einsum('qzm,qm->qz', down_factor_rows.astype(jnp.float32), attention_output.astype(jnp.float32)).astype(jnp.bfloat16)
    expand = jnp.einsum('tr,trd->td', reduced_features.astype(jnp.float32), up_factor_rows.astype(jnp.float32))
    return (base + expand).astype(jnp.bfloat16)
```

```python
import functools

import jax
import jax.numpy as jnp
from jax import lax
from jax.experimental import pallas as pl
from jax.experimental.pallas import tpu as pltpu
from jax.sharding import PartitionSpec as P

QUERY_HEADS = 64
F32, BF16 = jnp.float32, jnp.bfloat16
MESH = pl.DeviceIdType.MESH


def repeat(lo, hi, body):
    if hi - lo <= 8:
        for i in range(lo, hi):
            body(i)
    else:
        lax.fori_loop(lo, hi, lambda i, c: (body(i), c)[1], 0)


def gather_kernel(table, down, up, out_down, out_up, sems):
    resident = down.shape[0]
    copies = []
    for s in range(out_down.shape[0]):
        index = lax.rem(table[s], resident)
        copies.append(pltpu.make_async_copy(down.at[index], out_down.at[s], sems.at[0, s]))
        copies.append(pltpu.make_async_copy(up.at[index], out_up.at[s], sems.at[1, s]))
    for c in copies:
        c.start()
    for c in copies:
        c.wait()


def main_kernel(
    n, resident,
    length, slot, table, query, key_hbm, value_hbm, weight_hbm, down_hbm, up_hbm,
    out,
    key, value, weight, down, up,
    q_send, q_all, pay_send, pay_all, att_send, att_recv, code_send, code_recv,
    shr_send, shr_all, base_send, base_all, fin_own, fin_send, fin_recv,
    load_sem, w_sem, q_ss, q_rs, pay_ss, pay_rs, shr_ss, shr_rs, base_ss, base_rs, pair_ss, pair_rs,
):
    me = lax.axis_index("tensor")
    r = lax.axis_index("replica")
    requests, features = query.shape
    head = key.shape[3]
    kv_heads, span = key.shape[1], key.shape[2]
    own = features // head
    group = QUERY_HEADS // kv_heads
    rows = q_send.shape[0]
    width = weight.shape[2]
    split = width < features
    slots = down.shape[0]
    rank = down.shape[1]

    def peer(i):
        return lax.rem(me + i, n)

    def w_copy(i):
        p = peer(i)
        start = p * features + (r * width if split else 0)
        return pltpu.make_async_copy(
            weight_hbm.at[:, pl.ds(pl.multiple_of(start, 128), width)], weight.at[i % n], w_sem.at[i % n]
        )

    loads = [
        pltpu.make_async_copy(key_hbm, key, load_sem.at[0]),
        pltpu.make_async_copy(value_hbm, value, load_sem.at[1]),
        pltpu.make_async_copy(down_hbm, down, load_sem.at[2]),
        pltpu.make_async_copy(up_hbm, up, load_sem.at[3]),
    ]
    for c in loads[:3]:
        c.start()
    repeat(1, n + 1, lambda i: w_copy(i).start())
    loads[3].start()

    barrier = pltpu.get_barrier_semaphore()
    repeat(1, n, lambda i: pl.semaphore_signal(barrier, inc=1, device_id={"tensor": peer(i)}, device_id_type=MESH))
    pl.semaphore_signal(barrier, inc=1, device_id={"replica": 1 - r}, device_id_type=MESH)

    q = query[...].astype(F32)
    pieces = [q[:, h * head : (h + 1) * head] for h in range(own)]
    while len(pieces) * requests < rows:
        pieces.append(jnp.zeros_like(pieces[0]))
    q_send[...] = jnp.concatenate(pieces, axis=0).astype(BF16)

    row_of = lax.broadcasted_iota(jnp.int32, (requests, 128), 0)
    code_own = jnp.full((requests, 128), -1, jnp.int32)
    code_other = jnp.full((requests, 128), -1, jnp.int32)
    for t in range(requests):
        placed = r * (slots // 2) + slot[t]
        home = table[placed] // resident
        code_own = jnp.where(row_of == t, jnp.where(home == r, placed, -1), code_own)
        code_other = jnp.where(row_of == t, jnp.where(home == r, -1, placed), code_other)
    code_send[...] = code_other

    pl.semaphore_wait(barrier, n)

    def to_peer(src, dst, ss, rs, i):
        return pltpu.make_async_remote_copy(
            src_ref=src, dst_ref=dst.at[me], send_sem=ss.at[i], recv_sem=rs.at[me],
            device_id={"tensor": peer(i)}, device_id_type=MESH,
        )

    def from_peer(src, dst, ss, rs, i):
        p = peer(i)
        return pltpu.make_async_remote_copy(
            src_ref=src, dst_ref=dst.at[p], send_sem=ss.at[i], recv_sem=rs.at[p],
            device_id={"tensor": p}, device_id_type=MESH,
        )

    def to_pair(src, dst, k):
        return pltpu.make_async_remote_copy(
            src_ref=src, dst_ref=dst, send_sem=pair_ss.at[k], recv_sem=pair_rs.at[k],
            device_id={"replica": 1 - r}, device_id_type=MESH,
        )

    repeat(1, n, lambda i: to_peer(q_send, q_all, q_ss, q_rs, i).start())
    codes = to_pair(code_send, code_recv, 0)
    codes.start()

    columns = requests * span
    col = lax.broadcasted_iota(jnp.int32, (rows, columns), 1)
    row = lax.broadcasted_iota(jnp.int32, (rows, columns), 0)
    limit = jnp.zeros((rows, columns), jnp.int32)
    for t in range(requests):
        limit = jnp.where(col // span == t, length[t], limit)
    live = (lax.rem(row, requests) == col // span) & (me * span + lax.rem(col, span) < limit)
    eye = lax.broadcasted_iota(jnp.int32, (rows, 128), 0) == lax.broadcasted_iota(jnp.int32, (rows, 128), 1)
    stat_row = lax.broadcasted_iota(jnp.int32, (16, 128), 0)
    scale = 1.0 / (float(head) ** 0.5)

    loads[0].wait()
    loads[1].wait()

    def as_row(c):
        return jnp.sum(jnp.where(eye, c, 0.0), axis=0, keepdims=True)

    def attend(p, q_rows):
        kv = (p * own) // group
        k = key[:, kv].reshape(columns, head)
        v = value[:, kv].reshape(columns, head)
        score = lax.dot_general(q_rows, k, (((1,), (1,)), ((), ())), preferred_element_type=F32) * scale
        score = jnp.where(live, score, -1e30)
        top = jnp.max(score, axis=1, keepdims=True).astype(BF16).astype(F32)
        expo = jnp.where(live, jnp.exp(score - top), 0.0)
        total = jnp.sum(expo, axis=1, keepdims=True)
        summed = jnp.dot(expo.astype(BF16), v, preferred_element_type=F32)
        total_row = as_row(total)
        high = total_row.astype(BF16).astype(F32)
        stats = jnp.where(
            stat_row == 0, as_row(top), jnp.where(stat_row == 1, high, jnp.where(stat_row == 2, total_row - high, 0.0))
        )
        return summed.astype(BF16), stats.astype(BF16)

    summed, stats = attend(me, q_send[...])
    pay_all[me, 0:rows, :] = summed
    pay_all[me, rows : rows + 16, :] = stats

    def attend_step(i):
        from_peer(q_send, q_all, q_ss, q_rs, i).wait_recv()
        summed, stats = attend(peer(i), q_all[peer(i)])
        pay_send[i, 0:rows, :] = summed
        pay_send[i, rows : rows + 16, :] = stats
        to_peer(pay_send.at[i], pay_all, pay_ss, pay_rs, i).start()

    repeat(1, n, attend_step)
    repeat(1, n, lambda i: from_peer(pay_send.at[i], pay_all, pay_ss, pay_rs, i).wait_recv())

    stat = pay_all[:, rows : rows + 16, :].astype(F32)
    top = stat[:, 0, :]
    total = stat[:, 1, :] + stat[:, 2, :]
    factor = jnp.exp(top - jnp.max(top, axis=0, keepdims=True))
    share = factor / jnp.sum(factor * total, axis=0, keepdims=True)
    acc = jnp.zeros((rows, head), F32)
    for p in range(n):
        c = jnp.sum(jnp.where(eye, share[p : p + 1, :], 0.0), axis=1, keepdims=True)
        acc = acc + c * pay_all[p, 0:rows, :].astype(F32)
    att_send[...] = acc.astype(BF16)
    swap = to_pair(att_send, att_recv, 1)
    swap.start()

    def side_by_side(x):
        return jnp.concatenate([x[h * requests : (h + 1) * requests] for h in range(own)], axis=1)

    loads[2].wait()
    codes.wait()
    code = jnp.concatenate([code_own, code_recv[...]], axis=0)[:, 0:1]
    slot_of = lax.broadcasted_iota(jnp.int32, (2 * requests, slots * rank), 1) // rank
    picked = slot_of == code
    swap.wait()
    both = jnp.concatenate(
        [side_by_side(att_send[...].astype(F32)), side_by_side(att_recv[...].astype(F32))], axis=0
    ).astype(BF16)

    every = lax.dot_general(
        both, down[...].reshape(slots * rank, features), (((1,), (1,)), ((), ())), preferred_element_type=F32
    )
    every = jnp.where(picked, every, 0.0)
    part = every[:, 0:128]
    for j in range(1, slots * rank // 128):
        part = part + every[:, j * 128 : (j + 1) * 128]
    part = part + pltpu.roll(part, rank, 1)
    shr_send[...] = part
    shr_all[me] = part
    repeat(1, n, lambda i: to_peer(shr_send, shr_all, shr_ss, shr_rs, i).start())

    def base_step(i):
        w_copy(i).wait()
        base_send[i] = jnp.dot(both, weight[i], preferred_element_type=F32).astype(BF16)
        to_peer(base_send.at[i], base_all, base_ss, base_rs, i).start()

    repeat(1, n, base_step)
    w_copy(n).wait()
    base_all[me] = jnp.dot(both, weight[0], preferred_element_type=F32).astype(BF16)

    loads[3].wait()
    repeat(1, n, lambda i: from_peer(shr_send, shr_all, shr_ss, shr_rs, i).wait_recv())
    shrink = jnp.sum(shr_all[...], axis=0).astype(BF16).astype(F32)
    spread = jnp.concatenate([shrink] * (slots * rank // 128), axis=1)
    spread = jnp.where(picked, spread, 0.0).astype(BF16)
    expand = jnp.dot(spread, up[...].reshape(slots * rank, features), preferred_element_type=F32)
    fin_own[...] = expand[0:requests]
    fin_send[...] = expand[requests:]

    repeat(1, n, lambda i: from_peer(base_send.at[i], base_all, base_ss, base_rs, i).wait_recv())
    base = jnp.sum(base_all[...].astype(F32), axis=0)
    if split:
        half = pl.ds(pl.multiple_of(r * width, 128), width)
        fin_own[:, half] = fin_own[:, half] + base[0:requests]
        fin_send[:, half] = fin_send[:, half] + base[requests:]
    else:
        fin_own[...] = fin_own[...] + base[0:requests]
    last = to_pair(fin_send, fin_recv, 2)
    last.start()

    def drain(i):
        to_peer(q_send, q_all, q_ss, q_rs, i).wait_send()
        to_peer(pay_send.at[i], pay_all, pay_ss, pay_rs, i).wait_send()
        to_peer(shr_send, shr_all, shr_ss, shr_rs, i).wait_send()
        to_peer(base_send.at[i], base_all, base_ss, base_rs, i).wait_send()

    repeat(1, n, drain)
    last.wait()
    out[...] = (fin_own[...] + fin_recv[...]).astype(BF16)


def shards(n, query, key, value, length, weight, down, up, table, slot):
    requests, features = query.shape
    _, kv_heads, span, head = key.shape
    resident, rank, _ = down.shape
    slots = table.shape[0]
    rows = max(16, requests * (features // head))
    width = features // 2 if features % 256 == 0 else features
    smem = pl.BlockSpec(memory_space=pltpu.SMEM)
    vmem = pl.BlockSpec(memory_space=pltpu.VMEM)
    hbm = pl.BlockSpec(memory_space=pl.ANY)
    placed = jax.ShapeDtypeStruct((slots, rank, features), BF16)
    slot_down, slot_up = pl.pallas_call(
        gather_kernel,
        out_shape=(placed, placed),
        in_specs=[smem, hbm, hbm],
        out_specs=(hbm, hbm),
        scratch_shapes=[pltpu.SemaphoreType.DMA((2, slots))],
        name="gather_slots",
    )(table, down, up)
    dma = pltpu.SemaphoreType.DMA
    return pl.pallas_call(
        functools.partial(main_kernel, n, resident),
        out_shape=jax.ShapeDtypeStruct((requests, features), BF16),
        in_specs=[smem, smem, smem, vmem, hbm, hbm, hbm, hbm, hbm],
        out_specs=vmem,
        scratch_shapes=[
            pltpu.VMEM(key.shape, BF16),
            pltpu.VMEM(value.shape, BF16),
            pltpu.VMEM((n, features, width), BF16),
            pltpu.VMEM((slots, rank, features), BF16),
            pltpu.VMEM((slots, rank, features), BF16),
            pltpu.VMEM((rows, head), BF16),
            pltpu.VMEM((n, rows, head), BF16),
            pltpu.VMEM((n, rows + 16, head), BF16),
            pltpu.VMEM((n, rows + 16, head), BF16),
            pltpu.VMEM((rows, head), BF16),
            pltpu.VMEM((rows, head), BF16),
            pltpu.VMEM((requests, 128), jnp.int32),
            pltpu.VMEM((requests, 128), jnp.int32),
            pltpu.VMEM((2 * requests, 128), F32),
            pltpu.VMEM((n, 2 * requests, 128), F32),
            pltpu.VMEM((n, 2 * requests, width), BF16),
            pltpu.VMEM((n, 2 * requests, width), BF16),
            pltpu.VMEM((requests, features), F32),
            pltpu.VMEM((requests, features), F32),
            pltpu.VMEM((requests, features), F32),
            dma((4,)),
            dma((n,)),
            dma((n,)),
            dma((n,)),
            dma((n,)),
            dma((n,)),
            dma((n,)),
            dma((n,)),
            dma((n,)),
            dma((n,)),
            dma((3,)),
            dma((3,)),
        ],
        compiler_params=pltpu.CompilerParams(
            collective_id=0, has_side_effects=True, vmem_limit_bytes=48 * 1024 * 1024
        ),
        name="decode_block",
    )(length, slot, table, query, key, value, weight, slot_down, slot_up)


def solution(mesh):
    in_specs = (
        P(("groups", "replica"), "tensor"),
        P(("groups", "replica"), None, "tensor", None),
        P(("groups", "replica"), None, "tensor", None),
        P(("groups", "replica")),
        P("tensor", None),
        P("replica", None, "tensor"),
        P("replica", None, "tensor"),
        P("groups"),
        P(("groups", "replica")),
    )
    out_specs = P(("groups", "replica"), "tensor")
    body = functools.partial(shards, mesh.shape["tensor"])
    return jax.shard_map(body, mesh=mesh, in_specs=in_specs, out_specs=out_specs, check_vma=False)
```

```python
import functools

import jax
import jax.numpy as jnp
from jax import lax
from jax.experimental import pallas as pl
from jax.experimental.pallas import tpu as pltpu
from jax.sharding import PartitionSpec as P

QUERY_HEADS = 64
F32, BF16 = jnp.float32, jnp.bfloat16
MESH = pl.DeviceIdType.MESH


def repeat(lo, hi, body):
    if hi - lo <= 8:
        for i in range(lo, hi):
            body(i)
    else:
        lax.fori_loop(lo, hi, lambda i, c: (body(i), c)[1], 0)


def gather_kernel(table, down, up, out_down, out_up, sems):
    resident = down.shape[0]
    copies = []
    for s in range(out_down.shape[0]):
        index = lax.rem(table[s], resident)
        copies.append(pltpu.make_async_copy(down.at[index], out_down.at[s], sems.at[0, s]))
        copies.append(pltpu.make_async_copy(up.at[index], out_up.at[s], sems.at[1, s]))
    for c in copies:
        c.start()
    for c in copies:
        c.wait()


def main_kernel(
    n, resident,
    length, slot, table, query, key, value, weight_hbm, down, up,
    out,
    weight,
    q_send, q_all, pay_send, pay_all, att_send, att_recv, code_send, code_recv,
    shr_send, shr_all, base_send, base_all, fin_own, fin_send, fin_recv,
    w_sem, q_ss, q_rs, pay_ss, pay_rs, shr_ss, shr_rs, base_ss, base_rs, pair_ss, pair_rs,
):
    me = lax.axis_index("tensor")
    r = lax.axis_index("replica")
    requests, features = query.shape
    head = key.shape[3]
    kv_heads, span = key.shape[1], key.shape[2]
    own = features // head
    group = QUERY_HEADS // kv_heads
    rows = q_send.shape[0]
    width = weight.shape[2]
    split = width < features
    slots = down.shape[0]
    rank = down.shape[1]

    def peer(i):
        return lax.rem(me + i, n)

    def w_copy(i):
        p = peer(i)
        start = p * features + (r * width if split else 0)
        return pltpu.make_async_copy(
            weight_hbm.at[:, pl.ds(pl.multiple_of(start, 128), width)], weight.at[i % n], w_sem.at[i % n]
        )

    repeat(1, n + 1, lambda i: w_copy(i).start())

    barrier = pltpu.get_barrier_semaphore()
    repeat(1, n, lambda i: pl.semaphore_signal(barrier, inc=1, device_id={"tensor": peer(i)}, device_id_type=MESH))
    pl.semaphore_signal(barrier, inc=1, device_id={"replica": 1 - r}, device_id_type=MESH)

    q = query[...].astype(F32)
    pieces = [q[:, h * head : (h + 1) * head] for h in range(own)]
    while len(pieces) * requests < rows:
        pieces.append(jnp.zeros_like(pieces[0]))
    q_send[...] = jnp.concatenate(pieces, axis=0).astype(BF16)

    row_of = lax.broadcasted_iota(jnp.int32, (requests, 128), 0)
    code_own = jnp.full((requests, 128), -1, jnp.int32)
    code_other = jnp.full((requests, 128), -1, jnp.int32)
    for t in range(requests):
        placed = r * (slots // 2) + slot[t]
        home = table[placed] // resident
        code_own = jnp.where(row_of == t, jnp.where(home == r, placed, -1), code_own)
        code_other = jnp.where(row_of == t, jnp.where(home == r, -1, placed), code_other)
    code_send[...] = code_other

    pl.semaphore_wait(barrier, n)

    def to_peer(src, dst, ss, rs, i):
        return pltpu.make_async_remote_copy(
            src_ref=src, dst_ref=dst.at[me], send_sem=ss.at[i], recv_sem=rs.at[me],
            device_id={"tensor": peer(i)}, device_id_type=MESH,
        )

    def from_peer(src, dst, ss, rs, i):
        p = peer(i)
        return pltpu.make_async_remote_copy(
            src_ref=src, dst_ref=dst.at[p], send_sem=ss.at[i], recv_sem=rs.at[p],
            device_id={"tensor": p}, device_id_type=MESH,
        )

    def to_pair(src, dst, k):
        return pltpu.make_async_remote_copy(
            src_ref=src, dst_ref=dst, send_sem=pair_ss.at[k], recv_sem=pair_rs.at[k],
            device_id={"replica": 1 - r}, device_id_type=MESH,
        )

    repeat(1, n, lambda i: to_peer(q_send, q_all, q_ss, q_rs, i).start())
    codes = to_pair(code_send, code_recv, 0)
    codes.start()

    columns = requests * span
    col = lax.broadcasted_iota(jnp.int32, (rows, columns), 1)
    row = lax.broadcasted_iota(jnp.int32, (rows, columns), 0)
    limit = jnp.zeros((rows, columns), jnp.int32)
    for t in range(requests):
        limit = jnp.where(col // span == t, length[t], limit)
    live = (lax.rem(row, requests) == col // span) & (me * span + lax.rem(col, span) < limit)
    eye = lax.broadcasted_iota(jnp.int32, (rows, 128), 0) == lax.broadcasted_iota(jnp.int32, (rows, 128), 1)
    stat_row = lax.broadcasted_iota(jnp.int32, (16, 128), 0)
    scale = 1.0 / (float(head) ** 0.5)

    def as_row(c):
        return jnp.sum(jnp.where(eye, c, 0.0), axis=0, keepdims=True)

    def attend(p, q_rows):
        kv = (p * own) // group
        k = key[:, kv].reshape(columns, head)
        v = value[:, kv].reshape(columns, head)
        score = lax.dot_general(q_rows, k, (((1,), (1,)), ((), ())), preferred_element_type=F32) * scale
        score = jnp.where(live, score, -1e30)
        top = jnp.max(score, axis=1, keepdims=True).astype(BF16).astype(F32)
        expo = jnp.where(live, jnp.exp(score - top), 0.0)
        total = jnp.sum(expo, axis=1, keepdims=True)
        summed = jnp.dot(expo.astype(BF16), v, preferred_element_type=F32)
        total_row = as_row(total)
        high = total_row.astype(BF16).astype(F32)
        stats = jnp.where(
            stat_row == 0, as_row(top), jnp.where(stat_row == 1, high, jnp.where(stat_row == 2, total_row - high, 0.0))
        )
        return summed.astype(BF16), stats.astype(BF16)

    summed, stats = attend(me, q_send[...])
    pay_all[me, 0:rows, :] = summed
    pay_all[me, rows : rows + 16, :] = stats

    def attend_step(i):
        from_peer(q_send, q_all, q_ss, q_rs, i).wait_recv()
        summed, stats = attend(peer(i), q_all[peer(i)])
        pay_send[i, 0:rows, :] = summed
        pay_send[i, rows : rows + 16, :] = stats
        to_peer(pay_send.at[i], pay_all, pay_ss, pay_rs, i).start()

    repeat(1, n, attend_step)
    repeat(1, n, lambda i: from_peer(pay_send.at[i], pay_all, pay_ss, pay_rs, i).wait_recv())

    stat = pay_all[:, rows : rows + 16, :].astype(F32)
    top = stat[:, 0, :]
    total = stat[:, 1, :] + stat[:, 2, :]
    factor = jnp.exp(top - jnp.max(top, axis=0, keepdims=True))
    share = factor / jnp.sum(factor * total, axis=0, keepdims=True)
    acc = jnp.zeros((rows, head), F32)
    for p in range(n):
        c = jnp.sum(jnp.where(eye, share[p : p + 1, :], 0.0), axis=1, keepdims=True)
        acc = acc + c * pay_all[p, 0:rows, :].astype(F32)
    att_send[...] = acc.astype(BF16)
    swap = to_pair(att_send, att_recv, 1)
    swap.start()

    def side_by_side(x):
        return jnp.concatenate([x[h * requests : (h + 1) * requests] for h in range(own)], axis=1)

    codes.wait()
    code = jnp.concatenate([code_own, code_recv[...]], axis=0)[:, 0:1]
    slot_of = lax.broadcasted_iota(jnp.int32, (2 * requests, slots * rank), 1) // rank
    picked = slot_of == code
    swap.wait()
    both = jnp.concatenate(
        [side_by_side(att_send[...].astype(F32)), side_by_side(att_recv[...].astype(F32))], axis=0
    ).astype(BF16)

    every = lax.dot_general(
        both, down[...].reshape(slots * rank, features), (((1,), (1,)), ((), ())), preferred_element_type=F32
    )
    every = jnp.where(picked, every, 0.0)
    part = every[:, 0:128]
    for j in range(1, slots * rank // 128):
        part = part + every[:, j * 128 : (j + 1) * 128]
    part = part + pltpu.roll(part, rank, 1)
    shr_send[...] = part
    shr_all[me] = part
    repeat(1, n, lambda i: to_peer(shr_send, shr_all, shr_ss, shr_rs, i).start())

    def base_step(i):
        w_copy(i).wait()
        base_send[i] = jnp.dot(both, weight[i], preferred_element_type=F32).astype(BF16)
        to_peer(base_send.at[i], base_all, base_ss, base_rs, i).start()

    repeat(1, n, base_step)
    w_copy(n).wait()
    base_all[me] = jnp.dot(both, weight[0], preferred_element_type=F32).astype(BF16)

    repeat(1, n, lambda i: from_peer(shr_send, shr_all, shr_ss, shr_rs, i).wait_recv())
    shrink = jnp.sum(shr_all[...], axis=0).astype(BF16).astype(F32)
    spread = jnp.concatenate([shrink] * (slots * rank // 128), axis=1)
    spread = jnp.where(picked, spread, 0.0).astype(BF16)
    expand = jnp.dot(spread, up[...].reshape(slots * rank, features), preferred_element_type=F32)
    fin_own[...] = expand[0:requests]
    fin_send[...] = expand[requests:]

    repeat(1, n, lambda i: from_peer(base_send.at[i], base_all, base_ss, base_rs, i).wait_recv())
    base = jnp.sum(base_all[...].astype(F32), axis=0)
    if split:
        half = pl.ds(pl.multiple_of(r * width, 128), width)
        fin_own[:, half] = fin_own[:, half] + base[0:requests]
        fin_send[:, half] = fin_send[:, half] + base[requests:]
    else:
        fin_own[...] = fin_own[...] + base[0:requests]
    last = to_pair(fin_send, fin_recv, 2)
    last.start()

    def drain(i):
        to_peer(q_send, q_all, q_ss, q_rs, i).wait_send()
        to_peer(pay_send.at[i], pay_all, pay_ss, pay_rs, i).wait_send()
        to_peer(shr_send, shr_all, shr_ss, shr_rs, i).wait_send()
        to_peer(base_send.at[i], base_all, base_ss, base_rs, i).wait_send()

    repeat(1, n, drain)
    last.wait()
    out[...] = (fin_own[...] + fin_recv[...]).astype(BF16)


def shards(n, query, key, value, length, weight, down, up, table, slot):
    requests, features = query.shape
    _, kv_heads, span, head = key.shape
    resident, rank, _ = down.shape
    slots = table.shape[0]
    rows = max(16, requests * (features // head))
    width = features // 2 if features % 256 == 0 else features
    smem = pl.BlockSpec(memory_space=pltpu.SMEM)
    vmem = pl.BlockSpec(memory_space=pltpu.VMEM)
    hbm = pl.BlockSpec(memory_space=pl.ANY)
    placed = jax.ShapeDtypeStruct((slots, rank, features), BF16)
    slot_down, slot_up = pl.pallas_call(
        gather_kernel,
        out_shape=(placed, placed),
        in_specs=[smem, hbm, hbm],
        out_specs=(vmem, vmem),
        scratch_shapes=[pltpu.SemaphoreType.DMA((2, slots))],
        compiler_params=pltpu.CompilerParams(vmem_limit_bytes=40 * 1024 * 1024),
        name="gather_slots",
    )(table, down, up)
    dma = pltpu.SemaphoreType.DMA
    return pl.pallas_call(
        functools.partial(main_kernel, n, resident),
        out_shape=jax.ShapeDtypeStruct((requests, features), BF16),
        in_specs=[smem, smem, smem, vmem, vmem, vmem, hbm, vmem, vmem],
        out_specs=vmem,
        scratch_shapes=[
            pltpu.VMEM((n, features, width), BF16),
            pltpu.VMEM((rows, head), BF16),
            pltpu.VMEM((n, rows, head), BF16),
            pltpu.VMEM((n, rows + 16, head), BF16),
            pltpu.VMEM((n, rows + 16, head), BF16),
            pltpu.VMEM((rows, head), BF16),
            pltpu.VMEM((rows, head), BF16),
            pltpu.VMEM((requests, 128), jnp.int32),
            pltpu.VMEM((requests, 128), jnp.int32),
            pltpu.VMEM((2 * requests, 128), F32),
            pltpu.VMEM((n, 2 * requests, 128), F32),
            pltpu.VMEM((n, 2 * requests, width), BF16),
            pltpu.VMEM((n, 2 * requests, width), BF16),
            pltpu.VMEM((requests, features), F32),
            pltpu.VMEM((requests, features), F32),
            pltpu.VMEM((requests, features), F32),
            dma((n,)),
            dma((n,)),
            dma((n,)),
            dma((n,)),
            dma((n,)),
            dma((n,)),
            dma((n,)),
            dma((n,)),
            dma((n,)),
            dma((3,)),
            dma((3,)),
        ],
        compiler_params=pltpu.CompilerParams(
            collective_id=0, has_side_effects=True, vmem_limit_bytes=40 * 1024 * 1024
        ),
        name="decode_block",
    )(length, slot, table, query, key, value, weight, slot_down, slot_up)


def solution(mesh):
    in_specs = (
        P(("groups", "replica"), "tensor"),
        P(("groups", "replica"), None, "tensor", None),
        P(("groups", "replica"), None, "tensor", None),
        P(("groups", "replica")),
        P("tensor", None),
        P("replica", None, "tensor"),
        P("replica", None, "tensor"),
        P("groups"),
        P(("groups", "replica")),
    )
    out_specs = P(("groups", "replica"), "tensor")
    body = functools.partial(shards, mesh.shape["tensor"])
    return jax.shard_map(body, mesh=mesh, in_specs=in_specs, out_specs=out_specs, check_vma=False)
```

```python
import functools

import jax
import jax.numpy as jnp
from jax import lax
from jax.experimental import pallas as pl
from jax.experimental.pallas import tpu as pltpu
from jax.sharding import PartitionSpec as P

QUERY_HEADS = 64
F32, BF16 = jnp.float32, jnp.bfloat16
MESH = pl.DeviceIdType.MESH


def repeat(lo, hi, body):
    if hi - lo <= 8:
        for i in range(lo, hi):
            body(i)
    else:
        lax.fori_loop(lo, hi, lambda i, c: (body(i), c)[1], 0)


def gather_kernel(table, down, up, out_down, out_up, sems):
    resident = down.shape[0]
    r = lax.axis_index("replica")
    slots = out_down.shape[0]

    def copies(s):
        index = lax.rem(table[s], resident)
        return (
            pltpu.make_async_copy(down.at[index], out_down.at[s], sems.at[0, s]),
            pltpu.make_async_copy(up.at[index], out_up.at[s], sems.at[1, s]),
        )

    def at_home(s):
        return table[s] // resident == r

    for s in range(slots):

        @pl.when(at_home(s))
        def _():
            for c in copies(s):
                c.start()

    for s in range(slots):

        @pl.when(jnp.logical_not(at_home(s)))
        def _():
            out_down[s] = jnp.zeros(out_down.shape[1:], out_down.dtype)
            out_up[s] = jnp.zeros(out_up.shape[1:], out_up.dtype)

    for s in range(slots):

        @pl.when(at_home(s))
        def _():
            for c in copies(s):
                c.wait()


def main_kernel(
    n, resident,
    length, slot, table, query, key, value, weight_hbm, down, up,
    out,
    weight,
    q_send, q_all, pay_send, pay_all, att_send, att_recv, code_send, code_recv,
    shr_send, shr_all, base_send, base_all, fin_own, fin_send, fin_recv,
    w_sem, q_ss, q_rs, pay_ss, pay_rs, shr_ss, shr_rs, base_ss, base_rs, pair_ss, pair_rs,
):
    me = lax.axis_index("tensor")
    r = lax.axis_index("replica")
    requests, features = query.shape
    head = key.shape[3]
    kv_heads, span = key.shape[1], key.shape[2]
    own = features // head
    group = QUERY_HEADS // kv_heads
    rows = q_send.shape[0]
    width = weight.shape[2]
    split = width < features
    slots = down.shape[0]
    rank = down.shape[1]

    def peer(i):
        return lax.rem(me + i, n)

    def w_copy(i):
        p = peer(i)
        start = p * features + (r * width if split else 0)
        return pltpu.make_async_copy(
            weight_hbm.at[:, pl.ds(pl.multiple_of(start, 128), width)], weight.at[i % n], w_sem.at[i % n]
        )

    repeat(1, n + 1, lambda i: w_copy(i).start())

    barrier = pltpu.get_barrier_semaphore()
    repeat(1, n, lambda i: pl.semaphore_signal(barrier, inc=1, device_id={"tensor": peer(i)}, device_id_type=MESH))
    pl.semaphore_signal(barrier, inc=1, device_id={"replica": 1 - r}, device_id_type=MESH)

    q = query[...].astype(F32)
    pieces = [q[:, h * head : (h + 1) * head] for h in range(own)]
    while len(pieces) * requests < rows:
        pieces.append(jnp.zeros_like(pieces[0]))
    q_send[...] = jnp.concatenate(pieces, axis=0).astype(BF16)

    row_of = lax.broadcasted_iota(jnp.int32, (requests, 128), 0)
    code_own = jnp.full((requests, 128), -1, jnp.int32)
    code_other = jnp.full((requests, 128), -1, jnp.int32)
    for t in range(requests):
        placed = r * (slots // 2) + slot[t]
        home = table[placed] // resident
        code_own = jnp.where(row_of == t, jnp.where(home == r, placed, -1), code_own)
        code_other = jnp.where(row_of == t, jnp.where(home == r, -1, placed), code_other)
    code_send[...] = code_other

    pl.semaphore_wait(barrier, n)

    def to_peer(src, dst, ss, rs, i):
        return pltpu.make_async_remote_copy(
            src_ref=src, dst_ref=dst.at[me], send_sem=ss.at[i], recv_sem=rs.at[me],
            device_id={"tensor": peer(i)}, device_id_type=MESH,
        )

    def from_peer(src, dst, ss, rs, i):
        p = peer(i)
        return pltpu.make_async_remote_copy(
            src_ref=src, dst_ref=dst.at[p], send_sem=ss.at[i], recv_sem=rs.at[p],
            device_id={"tensor": p}, device_id_type=MESH,
        )

    def to_pair(src, dst, k):
        return pltpu.make_async_remote_copy(
            src_ref=src, dst_ref=dst, send_sem=pair_ss.at[k], recv_sem=pair_rs.at[k],
            device_id={"replica": 1 - r}, device_id_type=MESH,
        )

    repeat(1, n, lambda i: to_peer(q_send, q_all, q_ss, q_rs, i).start())
    codes = to_pair(code_send, code_recv, 0)
    codes.start()

    columns = requests * span
    col = lax.broadcasted_iota(jnp.int32, (rows, columns), 1)
    row = lax.broadcasted_iota(jnp.int32, (rows, columns), 0)
    limit = jnp.zeros((rows, columns), jnp.int32)
    for t in range(requests):
        limit = jnp.where(col // span == t, length[t], limit)
    live = (lax.rem(row, requests) == col // span) & (me * span + lax.rem(col, span) < limit)
    eye = lax.broadcasted_iota(jnp.int32, (rows, 128), 0) == lax.broadcasted_iota(jnp.int32, (rows, 128), 1)
    stat_row = lax.broadcasted_iota(jnp.int32, (16, 128), 0)
    scale = 1.0 / (float(head) ** 0.5)

    def as_row(c):
        return jnp.sum(jnp.where(eye, c, 0.0), axis=0, keepdims=True)

    def attend(p, q_rows):
        kv = (p * own) // group
        k = key[:, kv].reshape(columns, head)
        v = value[:, kv].reshape(columns, head)
        score = lax.dot_general(q_rows, k, (((1,), (1,)), ((), ())), preferred_element_type=F32) * scale
        score = jnp.where(live, score, -1e30)
        top = jnp.max(score, axis=1, keepdims=True).astype(BF16).astype(F32)
        expo = jnp.where(live, jnp.exp(score - top), 0.0)
        total = jnp.sum(expo, axis=1, keepdims=True)
        summed = jnp.dot(expo.astype(BF16), v, preferred_element_type=F32)
        total_row = as_row(total)
        high = total_row.astype(BF16).astype(F32)
        stats = jnp.where(
            stat_row == 0, as_row(top), jnp.where(stat_row == 1, high, jnp.where(stat_row == 2, total_row - high, 0.0))
        )
        return summed.astype(BF16), stats.astype(BF16)

    summed, stats = attend(me, q_send[...])
    pay_all[me, 0:rows, :] = summed
    pay_all[me, rows : rows + 16, :] = stats

    def attend_step(i):
        from_peer(q_send, q_all, q_ss, q_rs, i).wait_recv()
        summed, stats = attend(peer(i), q_all[peer(i)])
        pay_send[i, 0:rows, :] = summed
        pay_send[i, rows : rows + 16, :] = stats
        to_peer(pay_send.at[i], pay_all, pay_ss, pay_rs, i).start()

    repeat(1, n, attend_step)
    repeat(1, n, lambda i: from_peer(pay_send.at[i], pay_all, pay_ss, pay_rs, i).wait_recv())

    stat = pay_all[:, rows : rows + 16, :].astype(F32)
    top = stat[:, 0, :]
    total = stat[:, 1, :] + stat[:, 2, :]
    factor = jnp.exp(top - jnp.max(top, axis=0, keepdims=True))
    share = factor / jnp.sum(factor * total, axis=0, keepdims=True)
    acc = jnp.zeros((rows, head), F32)
    for p in range(n):
        c = jnp.sum(jnp.where(eye, share[p : p + 1, :], 0.0), axis=1, keepdims=True)
        acc = acc + c * pay_all[p, 0:rows, :].astype(F32)
    att_send[...] = acc.astype(BF16)
    swap = to_pair(att_send, att_recv, 1)
    swap.start()

    def side_by_side(x):
        return jnp.concatenate([x[h * requests : (h + 1) * requests] for h in range(own)], axis=1)

    codes.wait()
    code = jnp.concatenate([code_own, code_recv[...]], axis=0)[:, 0:1]
    slot_of = lax.broadcasted_iota(jnp.int32, (2 * requests, slots * rank), 1) // rank
    picked = slot_of == code
    swap.wait()
    both = jnp.concatenate(
        [side_by_side(att_send[...].astype(F32)), side_by_side(att_recv[...].astype(F32))], axis=0
    ).astype(BF16)

    every = lax.dot_general(
        both, down[...].reshape(slots * rank, features), (((1,), (1,)), ((), ())), preferred_element_type=F32
    )
    every = jnp.where(picked, every, 0.0)
    part = every[:, 0:128]
    for j in range(1, slots * rank // 128):
        part = part + every[:, j * 128 : (j + 1) * 128]
    part = part + pltpu.roll(part, rank, 1)
    shr_send[...] = part
    shr_all[me] = part
    repeat(1, n, lambda i: to_peer(shr_send, shr_all, shr_ss, shr_rs, i).start())

    def base_step(i):
        w_copy(i).wait()
        base_send[i] = jnp.dot(both, weight[i], preferred_element_type=F32).astype(BF16)
        to_peer(base_send.at[i], base_all, base_ss, base_rs, i).start()

    repeat(1, n, base_step)
    w_copy(n).wait()
    base_all[me] = jnp.dot(both, weight[0], preferred_element_type=F32).astype(BF16)

    repeat(1, n, lambda i: from_peer(shr_send, shr_all, shr_ss, shr_rs, i).wait_recv())
    shrink = jnp.sum(shr_all[...], axis=0).astype(BF16).astype(F32)
    spread = jnp.concatenate([shrink] * (slots * rank // 128), axis=1)
    spread = jnp.where(picked, spread, 0.0).astype(BF16)
    expand = jnp.dot(spread, up[...].reshape(slots * rank, features), preferred_element_type=F32)
    fin_own[...] = expand[0:requests]
    fin_send[...] = expand[requests:]

    repeat(1, n, lambda i: from_peer(base_send.at[i], base_all, base_ss, base_rs, i).wait_recv())
    base = jnp.sum(base_all[...].astype(F32), axis=0)
    if split:
        half = pl.ds(pl.multiple_of(r * width, 128), width)
        fin_own[:, half] = fin_own[:, half] + base[0:requests]
        fin_send[:, half] = fin_send[:, half] + base[requests:]
    else:
        fin_own[...] = fin_own[...] + base[0:requests]
    last = to_pair(fin_send, fin_recv, 2)
    last.start()

    def drain(i):
        to_peer(q_send, q_all, q_ss, q_rs, i).wait_send()
        to_peer(pay_send.at[i], pay_all, pay_ss, pay_rs, i).wait_send()
        to_peer(shr_send, shr_all, shr_ss, shr_rs, i).wait_send()
        to_peer(base_send.at[i], base_all, base_ss, base_rs, i).wait_send()

    repeat(1, n, drain)
    last.wait()
    out[...] = (fin_own[...] + fin_recv[...]).astype(BF16)


def shards(n, query, key, value, length, weight, down, up, table, slot):
    requests, features = query.shape
    _, kv_heads, span, head = key.shape
    resident, rank, _ = down.shape
    slots = table.shape[0]
    rows = max(16, requests * (features // head))
    width = features // 2 if features % 256 == 0 else features
    smem = pl.BlockSpec(memory_space=pltpu.SMEM)
    vmem = pl.BlockSpec(memory_space=pltpu.VMEM)
    hbm = pl.BlockSpec(memory_space=pl.ANY)
    placed = jax.ShapeDtypeStruct((slots, rank, features), BF16)
    slot_down, slot_up = pl.pallas_call(
        gather_kernel,
        out_shape=(placed, placed),
        in_specs=[smem, hbm, hbm],
        out_specs=(vmem, vmem),
        scratch_shapes=[pltpu.SemaphoreType.DMA((2, slots))],
        compiler_params=pltpu.CompilerParams(vmem_limit_bytes=40 * 1024 * 1024),
        name="gather_slots",
    )(table, down, up)
    dma = pltpu.SemaphoreType.DMA
    return pl.pallas_call(
        functools.partial(main_kernel, n, resident),
        out_shape=jax.ShapeDtypeStruct((requests, features), BF16),
        in_specs=[smem, smem, smem, vmem, vmem, vmem, hbm, vmem, vmem],
        out_specs=vmem,
        scratch_shapes=[
            pltpu.VMEM((n, features, width), BF16),
            pltpu.VMEM((rows, head), BF16),
            pltpu.VMEM((n, rows, head), BF16),
            pltpu.VMEM((n, rows + 16, head), BF16),
            pltpu.VMEM((n, rows + 16, head), BF16),
            pltpu.VMEM((rows, head), BF16),
            pltpu.VMEM((rows, head), BF16),
            pltpu.VMEM((requests, 128), jnp.int32),
            pltpu.VMEM((requests, 128), jnp.int32),
            pltpu.VMEM((2 * requests, 128), F32),
            pltpu.VMEM((n, 2 * requests, 128), F32),
            pltpu.VMEM((n, 2 * requests, width), BF16),
            pltpu.VMEM((n, 2 * requests, width), BF16),
            pltpu.VMEM((requests, features), F32),
            pltpu.VMEM((requests, features), F32),
            pltpu.VMEM((requests, features), F32),
            dma((n,)),
            dma((n,)),
            dma((n,)),
            dma((n,)),
            dma((n,)),
            dma((n,)),
            dma((n,)),
            dma((n,)),
            dma((n,)),
            dma((3,)),
            dma((3,)),
        ],
        compiler_params=pltpu.CompilerParams(
            collective_id=0, has_side_effects=True, vmem_limit_bytes=40 * 1024 * 1024
        ),
        name="decode_block",
    )(length, slot, table, query, key, value, weight, slot_down, slot_up)


def solution(mesh):
    in_specs = (
        P(("groups", "replica"), "tensor"),
        P(("groups", "replica"), None, "tensor", None),
        P(("groups", "replica"), None, "tensor", None),
        P(("groups", "replica")),
        P("tensor", None),
        P("replica", None, "tensor"),
        P("replica", None, "tensor"),
        P("groups"),
        P(("groups", "replica")),
    )
    out_specs = P(("groups", "replica"), "tensor")
    body = functools.partial(shards, mesh.shape["tensor"])
    return jax.shard_map(body, mesh=mesh, in_specs=in_specs, out_specs=out_specs, check_vma=False)
```

```python
import functools

import jax
import jax.numpy as jnp
from jax import lax
from jax.experimental import pallas as pl
from jax.experimental.pallas import tpu as pltpu
from jax.sharding import PartitionSpec as P

QUERY_HEADS = 64
F32, BF16 = jnp.float32, jnp.bfloat16
MESH = pl.DeviceIdType.MESH


def repeat(lo, hi, body):
    if hi - lo <= 8:
        for i in range(lo, hi):
            body(i)
    else:
        lax.fori_loop(lo, hi, lambda i, c: (body(i), c)[1], 0)


def gather_kernel(table, down, up, out_down, out_up, sems):
    resident = down.shape[0]
    r = lax.axis_index("replica")
    slots = out_down.shape[0]

    def copies(s):
        index = lax.rem(table[s], resident)
        return (
            pltpu.make_async_copy(down.at[index], out_down.at[s], sems.at[0, s]),
            pltpu.make_async_copy(up.at[index], out_up.at[s], sems.at[1, s]),
        )

    def at_home(s):
        return table[s] // resident == r

    for s in range(slots):

        @pl.when(at_home(s))
        def _():
            for c in copies(s):
                c.start()

    for s in range(slots):

        @pl.when(jnp.logical_not(at_home(s)))
        def _():
            out_down[s] = jnp.zeros(out_down.shape[1:], out_down.dtype)
            out_up[s] = jnp.zeros(out_up.shape[1:], out_up.dtype)

    for s in range(slots):

        @pl.when(at_home(s))
        def _():
            for c in copies(s):
                c.wait()


def main_kernel(
    n, resident,
    length, slot, table, query, key, value, weight_hbm, down, up,
    out,
    weight,
    q_send, q_all, pay_send, pay_all, att_send, att_recv, code_send, code_recv,
    shr_send, shr_all, base_send, base_all, fin_own, fin_send, fin_recv,
    w_sem, q_ss, q_rs, pay_ss, pay_rs, shr_ss, shr_rs, base_ss, base_rs, pair_ss, pair_rs,
):
    me = lax.axis_index("tensor")
    r = lax.axis_index("replica")
    requests, features = query.shape
    head = key.shape[3]
    kv_heads, span = key.shape[1], key.shape[2]
    own = features // head
    group = QUERY_HEADS // kv_heads
    rows = q_send.shape[0]
    width = weight.shape[2]
    split = width < features
    slots = down.shape[0]
    rank = down.shape[1]

    def peer(i):
        if n & (n - 1):
            return (me + i) % n
        step = i % n
        other, bit = 0, 1
        while bit < n:
            other = other + bit * ((me // bit + step // bit) % 2)
            bit *= 2
        return other

    def w_copy(i):
        p = peer(i)
        start = p * features + (r * width if split else 0)
        return pltpu.make_async_copy(
            weight_hbm.at[:, pl.ds(pl.multiple_of(start, 128), width)], weight.at[i % n], w_sem.at[i % n]
        )

    repeat(1, n + 1, lambda i: w_copy(i).start())

    barrier = pltpu.get_barrier_semaphore()
    repeat(1, n, lambda i: pl.semaphore_signal(barrier, inc=1, device_id={"tensor": peer(i)}, device_id_type=MESH))
    pl.semaphore_signal(barrier, inc=1, device_id={"replica": 1 - r}, device_id_type=MESH)

    q = query[...].astype(F32)
    pieces = [q[:, h * head : (h + 1) * head] for h in range(own)]
    while len(pieces) * requests < rows:
        pieces.append(jnp.zeros_like(pieces[0]))
    q_send[...] = jnp.concatenate(pieces, axis=0).astype(BF16)

    row_of = lax.broadcasted_iota(jnp.int32, (requests, 128), 0)
    code_own = jnp.full((requests, 128), -1, jnp.int32)
    code_other = jnp.full((requests, 128), -1, jnp.int32)
    for t in range(requests):
        placed = r * (slots // 2) + slot[t]
        home = table[placed] // resident
        code_own = jnp.where(row_of == t, jnp.where(home == r, placed, -1), code_own)
        code_other = jnp.where(row_of == t, jnp.where(home == r, -1, placed), code_other)
    code_send[...] = code_other

    pl.semaphore_wait(barrier, n)

    def to_peer(src, dst, ss, rs, i):
        return pltpu.make_async_remote_copy(
            src_ref=src, dst_ref=dst.at[me], send_sem=ss.at[i], recv_sem=rs.at[me],
            device_id={"tensor": peer(i)}, device_id_type=MESH,
        )

    def from_peer(src, dst, ss, rs, i):
        p = peer(i)
        return pltpu.make_async_remote_copy(
            src_ref=src, dst_ref=dst.at[p], send_sem=ss.at[i], recv_sem=rs.at[p],
            device_id={"tensor": p}, device_id_type=MESH,
        )

    def to_pair(src, dst, k):
        return pltpu.make_async_remote_copy(
            src_ref=src, dst_ref=dst, send_sem=pair_ss.at[k], recv_sem=pair_rs.at[k],
            device_id={"replica": 1 - r}, device_id_type=MESH,
        )

    repeat(1, n, lambda i: to_peer(q_send, q_all, q_ss, q_rs, i).start())
    codes = to_pair(code_send, code_recv, 0)
    codes.start()

    columns = requests * span
    col = lax.broadcasted_iota(jnp.int32, (rows, columns), 1)
    row = lax.broadcasted_iota(jnp.int32, (rows, columns), 0)
    limit = jnp.zeros((rows, columns), jnp.int32)
    for t in range(requests):
        limit = jnp.where(col // span == t, length[t], limit)
    live = (lax.rem(row, requests) == col // span) & (me * span + lax.rem(col, span) < limit)
    eye = lax.broadcasted_iota(jnp.int32, (rows, 128), 0) == lax.broadcasted_iota(jnp.int32, (rows, 128), 1)
    stat_row = lax.broadcasted_iota(jnp.int32, (16, 128), 0)
    scale = 1.0 / (float(head) ** 0.5)

    def as_row(c):
        return jnp.sum(jnp.where(eye, c, 0.0), axis=0, keepdims=True)

    def attend(p, q_rows):
        kv = (p * own) // group
        k = key[:, kv].reshape(columns, head)
        v = value[:, kv].reshape(columns, head)
        score = lax.dot_general(q_rows, k, (((1,), (1,)), ((), ())), preferred_element_type=F32) * scale
        score = jnp.where(live, score, -1e30)
        top = jnp.max(score, axis=1, keepdims=True).astype(BF16).astype(F32)
        expo = jnp.where(live, jnp.exp(score - top), 0.0)
        total = jnp.sum(expo, axis=1, keepdims=True)
        summed = jnp.dot(expo.astype(BF16), v, preferred_element_type=F32)
        total_row = as_row(total)
        high = total_row.astype(BF16).astype(F32)
        stats = jnp.where(
            stat_row == 0, as_row(top), jnp.where(stat_row == 1, high, jnp.where(stat_row == 2, total_row - high, 0.0))
        )
        return summed.astype(BF16), stats.astype(BF16)

    summed, stats = attend(me, q_send[...])
    pay_all[me, 0:rows, :] = summed
    pay_all[me, rows : rows + 16, :] = stats

    def attend_step(i):
        from_peer(q_send, q_all, q_ss, q_rs, i).wait_recv()
        summed, stats = attend(peer(i), q_all[peer(i)])
        pay_send[i, 0:rows, :] = summed
        pay_send[i, rows : rows + 16, :] = stats
        to_peer(pay_send.at[i], pay_all, pay_ss, pay_rs, i).start()

    repeat(1, n, attend_step)
    repeat(1, n, lambda i: from_peer(pay_send.at[i], pay_all, pay_ss, pay_rs, i).wait_recv())

    stat = pay_all[:, rows : rows + 16, :].astype(F32)
    top = stat[:, 0, :]
    total = stat[:, 1, :] + stat[:, 2, :]
    factor = jnp.exp(top - jnp.max(top, axis=0, keepdims=True))
    share = factor / jnp.sum(factor * total, axis=0, keepdims=True)
    acc = jnp.zeros((rows, head), F32)
    for p in range(n):
        c = jnp.sum(jnp.where(eye, share[p : p + 1, :], 0.0), axis=1, keepdims=True)
        acc = acc + c * pay_all[p, 0:rows, :].astype(F32)
    att_send[...] = acc.astype(BF16)
    swap = to_pair(att_send, att_recv, 1)
    swap.start()

    def side_by_side(x):
        return jnp.concatenate([x[h * requests : (h + 1) * requests] for h in range(own)], axis=1)

    codes.wait()
    code = jnp.concatenate([code_own, code_recv[...]], axis=0)[:, 0:1]
    slot_of = lax.broadcasted_iota(jnp.int32, (2 * requests, slots * rank), 1) // rank
    picked = slot_of == code
    swap.wait()
    both = jnp.concatenate(
        [side_by_side(att_send[...].astype(F32)), side_by_side(att_recv[...].astype(F32))], axis=0
    ).astype(BF16)

    every = lax.dot_general(
        both, down[...].reshape(slots * rank, features), (((1,), (1,)), ((), ())), preferred_element_type=F32
    )
    every = jnp.where(picked, every, 0.0)
    part = every[:, 0:128]
    for j in range(1, slots * rank // 128):
        part = part + every[:, j * 128 : (j + 1) * 128]
    part = part + pltpu.roll(part, rank, 1)
    high = part.astype(BF16).astype(F32)
    lane = lax.broadcasted_iota(jnp.int32, part.shape, 1)
    part = jnp.where(lane < rank, high, part - high).astype(BF16)
    shr_send[...] = part
    shr_all[me] = part
    repeat(1, n, lambda i: to_peer(shr_send, shr_all, shr_ss, shr_rs, i).start())

    def base_step(i):
        w_copy(i).wait()
        base_send[i] = jnp.dot(both, weight[i], preferred_element_type=F32).astype(BF16)
        to_peer(base_send.at[i], base_all, base_ss, base_rs, i).start()

    repeat(1, n, base_step)
    w_copy(n).wait()
    base_all[me] = jnp.dot(both, weight[0], preferred_element_type=F32).astype(BF16)

    repeat(1, n, lambda i: from_peer(shr_send, shr_all, shr_ss, shr_rs, i).wait_recv())
    shrink = jnp.sum(shr_all[...].astype(F32), axis=0)
    shrink = (shrink + pltpu.roll(shrink, rank, 1)).astype(BF16).astype(F32)
    spread = jnp.concatenate([shrink] * (slots * rank // 128), axis=1)
    spread = jnp.where(picked, spread, 0.0).astype(BF16)
    expand = jnp.dot(spread, up[...].reshape(slots * rank, features), preferred_element_type=F32)
    fin_own[...] = expand[0:requests]
    fin_send[...] = expand[requests:]

    repeat(1, n, lambda i: from_peer(base_send.at[i], base_all, base_ss, base_rs, i).wait_recv())
    base = jnp.sum(base_all[...].astype(F32), axis=0)
    if split:
        half = pl.ds(pl.multiple_of(r * width, 128), width)
        fin_own[:, half] = fin_own[:, half] + base[0:requests]
        fin_send[:, half] = fin_send[:, half] + base[requests:]
    else:
        fin_own[...] = fin_own[...] + base[0:requests]
    last = to_pair(fin_send, fin_recv, 2)
    last.start()

    def drain(i):
        to_peer(q_send, q_all, q_ss, q_rs, i).wait_send()
        to_peer(pay_send.at[i], pay_all, pay_ss, pay_rs, i).wait_send()
        to_peer(shr_send, shr_all, shr_ss, shr_rs, i).wait_send()
        to_peer(base_send.at[i], base_all, base_ss, base_rs, i).wait_send()

    repeat(1, n, drain)
    last.wait()
    out[...] = (fin_own[...] + fin_recv[...]).astype(BF16)


def shards(n, query, key, value, length, weight, down, up, table, slot):
    requests, features = query.shape
    _, kv_heads, span, head = key.shape
    resident, rank, _ = down.shape
    slots = table.shape[0]
    rows = max(16, requests * (features // head))
    width = features // 2 if features % 256 == 0 else features
    smem = pl.BlockSpec(memory_space=pltpu.SMEM)
    vmem = pl.BlockSpec(memory_space=pltpu.VMEM)
    hbm = pl.BlockSpec(memory_space=pl.ANY)
    placed = jax.ShapeDtypeStruct((slots, rank, features), BF16)
    slot_down, slot_up = pl.pallas_call(
        gather_kernel,
        out_shape=(placed, placed),
        in_specs=[smem, hbm, hbm],
        out_specs=(vmem, vmem),
        scratch_shapes=[pltpu.SemaphoreType.DMA((2, slots))],
        compiler_params=pltpu.CompilerParams(vmem_limit_bytes=40 * 1024 * 1024),
        name="gather_slots",
    )(table, down, up)
    dma = pltpu.SemaphoreType.DMA
    return pl.pallas_call(
        functools.partial(main_kernel, n, resident),
        out_shape=jax.ShapeDtypeStruct((requests, features), BF16),
        in_specs=[smem, smem, smem, vmem, vmem, vmem, hbm, vmem, vmem],
        out_specs=vmem,
        scratch_shapes=[
            pltpu.VMEM((n, features, width), BF16),
            pltpu.VMEM((rows, head), BF16),
            pltpu.VMEM((n, rows, head), BF16),
            pltpu.VMEM((n, rows + 16, head), BF16),
            pltpu.VMEM((n, rows + 16, head), BF16),
            pltpu.VMEM((rows, head), BF16),
            pltpu.VMEM((rows, head), BF16),
            pltpu.VMEM((requests, 128), jnp.int32),
            pltpu.VMEM((requests, 128), jnp.int32),
            pltpu.VMEM((2 * requests, 128), BF16),
            pltpu.VMEM((n, 2 * requests, 128), BF16),
            pltpu.VMEM((n, 2 * requests, width), BF16),
            pltpu.VMEM((n, 2 * requests, width), BF16),
            pltpu.VMEM((requests, features), F32),
            pltpu.VMEM((requests, features), F32),
            pltpu.VMEM((requests, features), F32),
            dma((n,)),
            dma((n,)),
            dma((n,)),
            dma((n,)),
            dma((n,)),
            dma((n,)),
            dma((n,)),
            dma((n,)),
            dma((n,)),
            dma((3,)),
            dma((3,)),
        ],
        compiler_params=pltpu.CompilerParams(
            collective_id=0, has_side_effects=True, vmem_limit_bytes=40 * 1024 * 1024
        ),
        name="decode_block",
    )(length, slot, table, query, key, value, weight, slot_down, slot_up)


def solution(mesh):
    in_specs = (
        P(("groups", "replica"), "tensor"),
        P(("groups", "replica"), None, "tensor", None),
        P(("groups", "replica"), None, "tensor", None),
        P(("groups", "replica")),
        P("tensor", None),
        P("replica", None, "tensor"),
        P("replica", None, "tensor"),
        P("groups"),
        P(("groups", "replica")),
    )
    out_specs = P(("groups", "replica"), "tensor")
    body = functools.partial(shards, mesh.shape["tensor"])
    return jax.shard_map(body, mesh=mesh, in_specs=in_specs, out_specs=out_specs, check_vma=False)
```

```python
import functools

import jax
import jax.numpy as jnp
from jax import lax
from jax.experimental import pallas as pl
from jax.experimental.pallas import tpu as pltpu
from jax.sharding import PartitionSpec as P

QUERY_HEADS = 64
F32, BF16 = jnp.float32, jnp.bfloat16
MESH = pl.DeviceIdType.MESH


def repeat(lo, hi, body):
    if hi - lo <= 8:
        for i in range(lo, hi):
            body(i)
    else:
        lax.fori_loop(lo, hi, lambda i, c: (body(i), c)[1], 0)


def gather_kernel(table, down, up, out_down, out_up, sems):
    resident = down.shape[0]
    r = lax.axis_index("replica")
    slots = out_down.shape[0]

    def copies(s):
        index = lax.rem(table[s], resident)
        return (
            pltpu.make_async_copy(down.at[index], out_down.at[s], sems.at[0, s]),
            pltpu.make_async_copy(up.at[index], out_up.at[s], sems.at[1, s]),
        )

    def at_home(s):
        return table[s] // resident == r

    for s in range(slots):

        @pl.when(at_home(s))
        def _():
            for c in copies(s):
                c.start()

    for s in range(slots):

        @pl.when(jnp.logical_not(at_home(s)))
        def _():
            out_down[s] = jnp.zeros(out_down.shape[1:], out_down.dtype)
            out_up[s] = jnp.zeros(out_up.shape[1:], out_up.dtype)

    for s in range(slots):

        @pl.when(at_home(s))
        def _():
            for c in copies(s):
                c.wait()


def main_kernel(
    n, resident,
    length, slot, table, query, key, value, weight_hbm, down, up,
    out,
    weight,
    q_send, q_all, pay_send, pay_all, att_send, att_recv, code_send, code_recv,
    shr_send, shr_all, base_send, base_all, fin_own, fin_send, fin_recv,
    w_sem, q_ss, q_rs, pay_ss, pay_rs, shr_ss, shr_rs, base_ss, base_rs, pair_ss, pair_rs,
):
    me = lax.axis_index("tensor")
    r = lax.axis_index("replica")
    requests, features = query.shape
    head = key.shape[3]
    kv_heads, span = key.shape[1], key.shape[2]
    own = features // head
    group = QUERY_HEADS // kv_heads
    rows = q_send.shape[0]
    width = weight.shape[2]
    split = width < features
    slots = down.shape[0]
    rank = down.shape[1]

    def peer(i):
        if n & (n - 1):
            return (me + i) % n
        step = i % n
        other, bit = 0, 1
        while bit < n:
            other = other + bit * ((me // bit + step // bit) % 2)
            bit *= 2
        return other

    def w_copy(i):
        p = peer(i)
        start = p * features + (r * width if split else 0)
        return pltpu.make_async_copy(
            weight_hbm.at[:, pl.ds(pl.multiple_of(start, 128), width)], weight.at[i % n], w_sem.at[i % n]
        )


    barrier = pltpu.get_barrier_semaphore()
    repeat(1, n, lambda i: pl.semaphore_signal(barrier, inc=1, device_id={"tensor": peer(i)}, device_id_type=MESH))
    pl.semaphore_signal(barrier, inc=1, device_id={"replica": 1 - r}, device_id_type=MESH)

    q = query[...].astype(F32)
    pieces = [q[:, h * head : (h + 1) * head] for h in range(own)]
    while len(pieces) * requests < rows:
        pieces.append(jnp.zeros_like(pieces[0]))
    q_send[...] = jnp.concatenate(pieces, axis=0).astype(BF16)

    row_of = lax.broadcasted_iota(jnp.int32, (requests, 128), 0)
    code_own = jnp.full((requests, 128), -1, jnp.int32)
    code_other = jnp.full((requests, 128), -1, jnp.int32)
    for t in range(requests):
        placed = r * (slots // 2) + slot[t]
        home = table[placed] // resident
        code_own = jnp.where(row_of == t, jnp.where(home == r, placed, -1), code_own)
        code_other = jnp.where(row_of == t, jnp.where(home == r, -1, placed), code_other)
    code_send[...] = code_other

    pl.semaphore_wait(barrier, n)

    def to_peer(src, dst, ss, rs, i):
        return pltpu.make_async_remote_copy(
            src_ref=src, dst_ref=dst.at[me], send_sem=ss.at[i], recv_sem=rs.at[me],
            device_id={"tensor": peer(i)}, device_id_type=MESH,
        )

    def from_peer(src, dst, ss, rs, i):
        p = peer(i)
        return pltpu.make_async_remote_copy(
            src_ref=src, dst_ref=dst.at[p], send_sem=ss.at[i], recv_sem=rs.at[p],
            device_id={"tensor": p}, device_id_type=MESH,
        )

    def to_pair(src, dst, k):
        return pltpu.make_async_remote_copy(
            src_ref=src, dst_ref=dst, send_sem=pair_ss.at[k], recv_sem=pair_rs.at[k],
            device_id={"replica": 1 - r}, device_id_type=MESH,
        )

    repeat(1, n, lambda i: to_peer(q_send, q_all, q_ss, q_rs, i).start())
    codes = to_pair(code_send, code_recv, 0)
    codes.start()
    repeat(1, n + 1, lambda i: w_copy(i).start())

    columns = requests * span
    col = lax.broadcasted_iota(jnp.int32, (rows, columns), 1)
    row = lax.broadcasted_iota(jnp.int32, (rows, columns), 0)
    limit = jnp.zeros((rows, columns), jnp.int32)
    for t in range(requests):
        limit = jnp.where(col // span == t, length[t], limit)
    live = (lax.rem(row, requests) == col // span) & (me * span + lax.rem(col, span) < limit)
    eye = lax.broadcasted_iota(jnp.int32, (rows, 128), 0) == lax.broadcasted_iota(jnp.int32, (rows, 128), 1)
    stat_row = lax.broadcasted_iota(jnp.int32, (16, 128), 0)
    scale = 1.0 / (float(head) ** 0.5)

    def as_row(c):
        return jnp.sum(jnp.where(eye, c, 0.0), axis=0, keepdims=True)

    def attend(p, q_rows):
        kv = (p * own) // group
        k = key[:, kv].reshape(columns, head)
        v = value[:, kv].reshape(columns, head)
        score = lax.dot_general(q_rows, k, (((1,), (1,)), ((), ())), preferred_element_type=F32) * scale
        score = jnp.where(live, score, -1e30)
        top = jnp.max(score, axis=1, keepdims=True).astype(BF16).astype(F32)
        expo = jnp.where(live, jnp.exp(score - top), 0.0)
        total = jnp.sum(expo, axis=1, keepdims=True)
        summed = jnp.dot(expo.astype(BF16), v, preferred_element_type=F32)
        total_row = as_row(total)
        high = total_row.astype(BF16).astype(F32)
        stats = jnp.where(
            stat_row == 0, as_row(top), jnp.where(stat_row == 1, high, jnp.where(stat_row == 2, total_row - high, 0.0))
        )
        return summed.astype(BF16), stats.astype(BF16)

    summed, stats = attend(me, q_send[...])
    pay_all[me, 0:rows, :] = summed
    pay_all[me, rows : rows + 16, :] = stats

    def attend_step(i):
        from_peer(q_send, q_all, q_ss, q_rs, i).wait_recv()
        summed, stats = attend(peer(i), q_all[peer(i)])
        pay_send[i, 0:rows, :] = summed
        pay_send[i, rows : rows + 16, :] = stats
        to_peer(pay_send.at[i], pay_all, pay_ss, pay_rs, i).start()

    repeat(1, n, attend_step)
    repeat(1, n, lambda i: from_peer(pay_send.at[i], pay_all, pay_ss, pay_rs, i).wait_recv())

    stat = pay_all[:, rows : rows + 16, :].astype(F32)
    top = stat[:, 0, :]
    total = stat[:, 1, :] + stat[:, 2, :]
    factor = jnp.exp(top - jnp.max(top, axis=0, keepdims=True))
    share = factor / jnp.sum(factor * total, axis=0, keepdims=True)
    acc = jnp.zeros((rows, head), F32)
    for p in range(n):
        c = jnp.sum(jnp.where(eye, share[p : p + 1, :], 0.0), axis=1, keepdims=True)
        acc = acc + c * pay_all[p, 0:rows, :].astype(F32)
    att_send[...] = acc.astype(BF16)
    swap = to_pair(att_send, att_recv, 1)
    swap.start()

    def side_by_side(x):
        return jnp.concatenate([x[h * requests : (h + 1) * requests] for h in range(own)], axis=1)

    codes.wait()
    code = jnp.concatenate([code_own, code_recv[...]], axis=0)[:, 0:1]
    slot_of = lax.broadcasted_iota(jnp.int32, (2 * requests, slots * rank), 1) // rank
    picked = slot_of == code
    swap.wait()
    both = jnp.concatenate(
        [side_by_side(att_send[...].astype(F32)), side_by_side(att_recv[...].astype(F32))], axis=0
    ).astype(BF16)

    every = lax.dot_general(
        both, down[...].reshape(slots * rank, features), (((1,), (1,)), ((), ())), preferred_element_type=F32
    )
    every = jnp.where(picked, every, 0.0)
    part = every[:, 0:128]
    for j in range(1, slots * rank // 128):
        part = part + every[:, j * 128 : (j + 1) * 128]
    part = part + pltpu.roll(part, rank, 1)
    high = part.astype(BF16).astype(F32)
    lane = lax.broadcasted_iota(jnp.int32, part.shape, 1)
    part = jnp.where(lane < rank, high, part - high).astype(BF16)
    shr_send[...] = part
    shr_all[me] = part
    repeat(1, n, lambda i: to_peer(shr_send, shr_all, shr_ss, shr_rs, i).start())

    def base_step(i):
        w_copy(i).wait()
        base_send[i] = jnp.dot(both, weight[i], preferred_element_type=F32).astype(BF16)
        to_peer(base_send.at[i], base_all, base_ss, base_rs, i).start()

    repeat(1, n, base_step)
    w_copy(n).wait()
    base_all[me] = jnp.dot(both, weight[0], preferred_element_type=F32).astype(BF16)

    repeat(1, n, lambda i: from_peer(shr_send, shr_all, shr_ss, shr_rs, i).wait_recv())
    shrink = jnp.sum(shr_all[...].astype(F32), axis=0)
    shrink = (shrink + pltpu.roll(shrink, rank, 1)).astype(BF16).astype(F32)
    spread = jnp.concatenate([shrink] * (slots * rank // 128), axis=1)
    spread = jnp.where(picked, spread, 0.0).astype(BF16)
    expand = jnp.dot(spread, up[...].reshape(slots * rank, features), preferred_element_type=F32)
    fin_own[...] = expand[0:requests]
    fin_send[...] = expand[requests:]

    repeat(1, n, lambda i: from_peer(base_send.at[i], base_all, base_ss, base_rs, i).wait_recv())
    base = jnp.sum(base_all[...].astype(F32), axis=0)
    if split:
        half = pl.ds(pl.multiple_of(r * width, 128), width)
        fin_own[:, half] = fin_own[:, half] + base[0:requests]
        fin_send[:, half] = fin_send[:, half] + base[requests:]
    else:
        fin_own[...] = fin_own[...] + base[0:requests]
    last = to_pair(fin_send, fin_recv, 2)
    last.start()

    def drain(i):
        to_peer(q_send, q_all, q_ss, q_rs, i).wait_send()
        to_peer(pay_send.at[i], pay_all, pay_ss, pay_rs, i).wait_send()
        to_peer(shr_send, shr_all, shr_ss, shr_rs, i).wait_send()
        to_peer(base_send.at[i], base_all, base_ss, base_rs, i).wait_send()

    repeat(1, n, drain)
    last.wait()
    out[...] = (fin_own[...] + fin_recv[...]).astype(BF16)


def shards(n, query, key, value, length, weight, down, up, table, slot):
    requests, features = query.shape
    _, kv_heads, span, head = key.shape
    resident, rank, _ = down.shape
    slots = table.shape[0]
    rows = max(16, requests * (features // head))
    width = features // 2 if features % 256 == 0 else features
    smem = pl.BlockSpec(memory_space=pltpu.SMEM)
    vmem = pl.BlockSpec(memory_space=pltpu.VMEM)
    hbm = pl.BlockSpec(memory_space=pl.ANY)
    placed = jax.ShapeDtypeStruct((slots, rank, features), BF16)
    slot_down, slot_up = pl.pallas_call(
        gather_kernel,
        out_shape=(placed, placed),
        in_specs=[smem, hbm, hbm],
        out_specs=(vmem, vmem),
        scratch_shapes=[pltpu.SemaphoreType.DMA((2, slots))],
        compiler_params=pltpu.CompilerParams(vmem_limit_bytes=40 * 1024 * 1024),
        name="gather_slots",
    )(table, down, up)
    dma = pltpu.SemaphoreType.DMA
    return pl.pallas_call(
        functools.partial(main_kernel, n, resident),
        out_shape=jax.ShapeDtypeStruct((requests, features), BF16),
        in_specs=[smem, smem, smem, vmem, vmem, vmem, hbm, vmem, vmem],
        out_specs=vmem,
        scratch_shapes=[
            pltpu.VMEM((n, features, width), BF16),
            pltpu.VMEM((rows, head), BF16),
            pltpu.VMEM((n, rows, head), BF16),
            pltpu.VMEM((n, rows + 16, head), BF16),
            pltpu.VMEM((n, rows + 16, head), BF16),
            pltpu.VMEM((rows, head), BF16),
            pltpu.VMEM((rows, head), BF16),
            pltpu.VMEM((requests, 128), jnp.int32),
            pltpu.VMEM((requests, 128), jnp.int32),
            pltpu.VMEM((2 * requests, 128), BF16),
            pltpu.VMEM((n, 2 * requests, 128), BF16),
            pltpu.VMEM((n, 2 * requests, width), BF16),
            pltpu.VMEM((n, 2 * requests, width), BF16),
            pltpu.VMEM((requests, features), F32),
            pltpu.VMEM((requests, features), F32),
            pltpu.VMEM((requests, features), F32),
            dma((n,)),
            dma((n,)),
            dma((n,)),
            dma((n,)),
            dma((n,)),
            dma((n,)),
            dma((n,)),
            dma((n,)),
            dma((n,)),
            dma((3,)),
            dma((3,)),
        ],
        compiler_params=pltpu.CompilerParams(
            collective_id=0, has_side_effects=True, vmem_limit_bytes=40 * 1024 * 1024
        ),
        name="decode_block",
    )(length, slot, table, query, key, value, weight, slot_down, slot_up)


def solution(mesh):
    in_specs = (
        P(("groups", "replica"), "tensor"),
        P(("groups", "replica"), None, "tensor", None),
        P(("groups", "replica"), None, "tensor", None),
        P(("groups", "replica")),
        P("tensor", None),
        P("replica", None, "tensor"),
        P("replica", None, "tensor"),
        P("groups"),
        P(("groups", "replica")),
    )
    out_specs = P(("groups", "replica"), "tensor")
    body = functools.partial(shards, mesh.shape["tensor"])
    return jax.shard_map(body, mesh=mesh, in_specs=in_specs, out_specs=out_specs, check_vma=False)
```
